256 devices in a mesh: row: 16 (over z, core), col: 16 (over y, x).
Axes of the slice: x: 4, y: 4, z: 8, core: 2. Of those that a mesh axis runs over, the one named last changes fastest.
Arguments:
- node_input: bfloat16 [32768, 128], P(('row', 'col')), may hold values from -6 to 6
- adj_tiles: bfloat16 [16, 16, 128, 128, 128], P('row', 'col'), may hold values from -0.046875 to 0.046875
- tile_row: int32 [16, 16, 128], P('row', 'col'), may hold values from 0 to 15
- tile_col: int32 [16, 16, 128], P('row', 'col'), may hold values from 0 to 15
- weight_in: bfloat16 [128, 512], replicated, may hold values from -0.5 to 0.5
- weight_out: bfloat16 [512, 128], replicated, may hold values from -0.25 to 0.25
- logit_grad: bfloat16 [32768, 128], P(('row', 'col')), may hold values from -6 to 6
Outputs:
- logits: float32 [32768, 128], P(('row', 'col'))
- w_in_grad: float32 [128, 512], replicated
- w_out_grad: float32 [512, 128], replicated
The draws below stay inside these ranges and needn't reach their ends.
Inputs may be any that keep to these rules, and one draw needn't show every extreme that they name: tile_row[r, c, k] names the tile of nodes within block row r: the nodes 128 * (r * 16 + tile_row) onward; a device's tiles may repeat a position. tile_col[r, c, k] = q names the tile of nodes 128 * (q * 16 + c) onward; some columns are named far more often than others.
All inputs are finite; a program needn't handle non-finite values.
Results may differ from the reference program's by a relative error of at most 0.0045.
Values may be sent and summed in bfloat16 or wider, within the bound.
No kernel may reach another device: no remote copies, remote signals or barrier semaphores. Data moves between devices by JAX's collectives and lax.ppermute only.
A program may use at most 128 MiB of HBM per device.

```python
import math
import jax
import jax.numpy as jnp
import numpy as np
from jax import lax

TILE = 128
TB_DEV = 1
TILES_DEV = 128
F_IN = 128
HID = 512
F_OUT = 128
NODES = 32768
N_ROW = 16
N_COL = 16


def set_ends(drawn, key, low, high):
    shape = drawn.shape
    index_at = [jax.random.randint(jax.random.fold_in(key, axis), (), 0, shape[axis]) for axis in range(len(shape))]
    drawn = drawn.at[tuple(index_at)].set(low)
    longest = shape.index(max(shape))
    index_at[longest] = (index_at[longest] + 1) % shape[longest]
    return drawn.at[tuple(index_at)].set(high)


def level_of(stream_key, dims, shards, smallest, largest):
    gain, own = 1.0, jax.random.fold_in(stream_key, 6)
    for axis_at, blocks in shards:
        steps = jnp.exp(jax.random.uniform(jax.random.fold_in(own, axis_at), (blocks,), jnp.float32, smallest / len(shards), largest / len(shards)))
        gain = gain * jnp.repeat(steps, dims[axis_at] // blocks).reshape([-1 if axis == axis_at else 1 for axis in range(len(dims))])
    return gain


def cumulative_ranks(count, slope):
    loads = [(1 << 20) // math.isqrt(grade ** slope) + 1 for grade in range(1, count + 1)]
    deviation = 1 + sum(loads) // (1 << 30)
    return np.cumsum(np.array([max(1, weight // deviation) for weight in loads]))


def ranked(rng, dims, count, lean):
    listing = cumulative_ranks(count, lean)
    lot = jax.random.randint(jax.random.fold_in(rng, 1), dims, 0, int(listing[count - 1]))
    standing = jnp.searchsorted(jnp.asarray(listing, jnp.int32), lot, side="right")
    return jax.random.permutation(jax.random.fold_in(rng, 2), count)[standing].astype(jnp.int32)


def bell_draw(stream_key, extent, width, limit, pieces=(), held_as=jnp.bfloat16):
    result = jax.random.normal(stream_key, extent, jnp.float32) * width
    if len(pieces) > 0:
        result = level_of(stream_key, extent, pieces, -0.22, 0.18) * result
    return jnp.clip(result, min=-limit, max=limit).astype(held_as)


def setup_inputs(seed: int = 0) -> dict:
    seeds = jax.random.split(jax.random.key(seed), 8)
    return {
        "node_input": bell_draw(seeds[0], (NODES, F_IN), 1.0, 6.0, ((0, 256),)),
        "adj_tiles": bell_draw(seeds[1], (N_ROW, N_COL, TILES_DEV, TILE, TILE), (TILES_DEV * TILE // TB_DEV) ** -0.5, 0.046875, ((0, 16), (1, 16))),
        "tile_row": set_ends(jax.random.randint(seeds[2], (N_ROW, N_COL, TILES_DEV), 0, TB_DEV * N_COL), jax.random.fold_in(seeds[2], 1), 0, (TB_DEV * N_COL) - 1).astype(jnp.int32),
        "tile_col": set_ends(ranked(seeds[3], (N_ROW, N_COL, TILES_DEV), TB_DEV * N_ROW, 2), jax.random.fold_in(seeds[3], 3), 0, (TB_DEV * N_ROW) - 1).astype(jnp.int32),
        "weight_in": bell_draw(seeds[4], (F_IN, HID), F_IN ** -0.5, 0.5),
        "weight_out": bell_draw(seeds[5], (HID, F_OUT), HID ** -0.5, 0.25),
        "logit_grad": bell_draw(seeds[6], (NODES, F_OUT), 1.0, 6.0, ((0, 256),)),
    }


def spread_tiles(tile_vals, target_ids, source_ids, features, out_tiles, transpose):
    tile_size = tile_vals.shape[-1]
    feat_width = features.shape[-1]
    blocks = features.reshape(-1, tile_size, feat_width).astype(jnp.float32)
    tile_total = tile_vals.shape[0]
    block_size = math.gcd(tile_total, 16)
    pattern = 'tji,tjf->tif' if transpose else 'tij,tjf->tif'

    def add_block(totals, block_number):
        first_tile = block_number * block_size
        chosen = lax.dynamic_slice_in_dim(tile_vals, first_tile, block_size, 0).astype(jnp.float32)
        target = lax.dynamic_slice_in_dim(target_ids, first_tile, block_size, 0)
        source = lax.dynamic_slice_in_dim(source_ids, first_tile, block_size, 0)
        picked = blocks[source]
        product = jnp.einsum(pattern, chosen, picked, precision=lax.Precision.HIGHEST)
        return (totals.at[target].add(product), None)
    totals = jnp.zeros((out_tiles, tile_size, feat_width), jnp.float32)
    totals, _ = lax.scan(add_block, totals, jnp.arange(tile_total // block_size, dtype=jnp.int32))
    return totals.reshape(out_tiles * tile_size, feat_width)

def reference(node_input, adj_tiles, tile_row, tile_col, weight_in, weight_out, logit_grad):
    row_base = (jnp.arange(N_ROW, dtype=jnp.int32) * (N_COL * TB_DEV))[:, None, None]
    col_base = (jnp.arange(N_COL, dtype=jnp.int32) * TB_DEV)[None, :, None]
    global_rows = (row_base + tile_row).reshape(-1).astype(jnp.int32)
    global_cols = (tile_col // TB_DEV * (N_COL * TB_DEV) + col_base + tile_col % TB_DEV).reshape(-1).astype(jnp.int32)
    tile_vals = adj_tiles.reshape(-1, TILE, TILE)
    node_tiles = NODES // TILE
    scale = 1.0 / math.sqrt(NODES)
    agg_in = spread_tiles(tile_vals, global_rows, global_cols, node_input, node_tiles, False).astype(jnp.bfloat16)
    pre_act = jnp.dot(agg_in, weight_in, preferred_element_type=jnp.float32)
    hidden = jax.nn.silu(pre_act).astype(jnp.bfloat16)
    out_weight = weight_out.astype(jnp.float32)
    projected = jnp.dot(hidden, weight_out, preferred_element_type=jnp.float32)
    logits = spread_tiles(tile_vals, global_rows, global_cols, projected, node_tiles, False)
    pulled = spread_tiles(tile_vals, global_cols, global_rows, logit_grad, node_tiles, True) * scale
    grad_hidden = jnp.dot(pulled, out_weight.T, precision=lax.Precision.HIGHEST)
    w_out_grad = jnp.dot(hidden.astype(jnp.float32).T, pulled, precision=lax.Precision.HIGHEST)
    sigmoid_vals = jax.nn.sigmoid(pre_act)
    grad_pre = grad_hidden * sigmoid_vals * (1.0 + pre_act * (1.0 - sigmoid_vals))
    w_in_grad = jnp.dot(agg_in.astype(jnp.float32).T, grad_pre, precision=lax.Precision.HIGHEST)
    return (logits, w_in_grad, w_out_grad)
```

```python
import functools
import math

import jax
import jax.numpy as jnp
from jax import lax
from jax.experimental import pallas as pl
from jax.experimental.pallas import tpu as pltpu
from jax.sharding import PartitionSpec as P

B, F = jnp.bfloat16, jnp.float32
VMEM = pl.BlockSpec(memory_space=pltpu.VMEM)
SMEM = pl.BlockSpec(memory_space=pltpu.SMEM)
T = 128
G = 16
UNROLL = 32


def kernel_call(body, out, specs, scratch, flops, name):
    return pl.pallas_call(
        body,
        out_shape=out,
        in_specs=specs,
        out_specs=jax.tree.map(lambda _: VMEM, out),
        scratch_shapes=scratch,
        cost_estimate=pl.CostEstimate(flops=flops, bytes_accessed=6 << 20, transcendentals=0),
        compiler_params=pltpu.CompilerParams(vmem_limit_bytes=40 << 20),
        name=name,
    )


def each_tile(total, count, product, target):
    def step(block, carry):
        first = block * UNROLL
        parts = [product(first + u) for u in range(UNROLL)]
        for u in range(UNROLL):
            total[target(first + u)] += parts[u]
        return carry

    lax.fori_loop(0, count // UNROLL, step, 0)


def spread_first(rows, cols, tiles, feats, grads, out, total):
    total[...] = jnp.zeros_like(total)
    each_tile(
        total,
        tiles.shape[0],
        lambda k: jnp.dot(tiles[k], feats[cols[k]], preferred_element_type=F),
        lambda k: rows[k],
    )
    for i in range(G):
        value = total[i]
        high = value.astype(B)
        out[i, 0:T] = high
        out[i, T : 2 * T] = (value - high.astype(F)).astype(B)
        out[i, 2 * T : 3 * T] = grads[...]


def spread_second(rows, cols, tiles, feats, out, total):
    total[...] = jnp.zeros_like(total)
    each_tile(
        total,
        tiles.shape[0],
        lambda k: jnp.dot(tiles[k], feats[cols[k]], preferred_element_type=F),
        lambda k: rows[k],
    )
    for i in range(G):
        out[i, 0:T] = total[i].astype(B)
        out[i, T:] = jnp.zeros((out.shape[1] - T, T), B)


def spread_back(rows, cols, tiles, received, out, turned):
    for i in range(G):
        turned[i] = received[i, 2 * T : 3 * T].T
    out[...] = jnp.zeros_like(out)
    each_tile(
        out,
        tiles.shape[0],
        lambda k: jnp.dot(turned[rows[k]], tiles[k], preferred_element_type=F),
        lambda k: cols[k],
    )


def dense_part(scale, agg, pulled, w_in, w_out, w_out_t, proj, packed, in_sum, out_sum):
    in_sum[...] = jnp.zeros_like(in_sum)
    out_sum[...] = jnp.zeros_like(out_sum)

    def step(q, carry):
        nodes = agg[q]
        pre = jnp.dot(nodes, w_in[...], preferred_element_type=F)
        sig = jax.nn.sigmoid(pre)
        act = pre * sig
        hidden = act.astype(B)
        proj[q] = jnp.dot(hidden, w_out[...], preferred_element_type=F).astype(B)
        back = (pulled[q] * scale).astype(B)
        grad = lax.dot_general(
            back, w_out_t[...], (((0,), (0,)), ((), ())), preferred_element_type=F
        )
        grad_pre = grad * sig * (1.0 + pre * (1.0 - sig))
        in_sum[...] += lax.dot_general(
            nodes, grad_pre.astype(B), (((0,), (0,)), ((), ())), preferred_element_type=F
        )
        out_sum[...] += jnp.dot(back, hidden, preferred_element_type=F)
        return carry

    lax.fori_loop(0, G, step, 0)
    out_grad = out_sum[...].T
    for s in range(G):
        parts = [in_sum[8 * s : 8 * s + 8, T * b : T * b + T] for b in range(4)]
        parts.append(out_grad[32 * s : 32 * s + 32])
        packed[s] = jnp.concatenate(parts, 0).astype(B)


def unpack(slices, in_grad, out_grad):
    for s in range(G):
        piece = slices[s % 2, s // 2].astype(F)
        for b in range(4):
            in_grad[8 * s : 8 * s + 8, T * b : T * b + T] = piece[8 * b : 8 * b + 8]
        out_grad[32 * s : 32 * s + 32] = piece[32:64]


def swap(value, axis, groups=None):
    return lax.all_to_all(value, axis, 0, 0, tiled=True, axis_index_groups=groups)


def gather_row(value):
    same_core = [[2 * z + core for z in range(G // 2)] for core in range(2)]
    same_chip = [[2 * z, 2 * z + 1] for z in range(G // 2)]
    along_z = swap(jnp.broadcast_to(value[None], (G // 2,) + value.shape), "row", same_core)
    return lax.all_gather(along_z, "row", axis=0, axis_index_groups=same_chip)


def on_device(node_input, adj_tiles, tile_row, tile_col, weight_in, weight_out, logit_grad):
    tiles = adj_tiles.reshape(-1, T, T)
    rows = tile_row.reshape(-1)
    cols = tile_col.reshape(-1)
    cols = (cols % 2) * (G // 2) + cols // 2
    node_total = node_input.shape[0] * G * G
    scale = 1.0 / math.sqrt(node_total)
    spread_flops = 2 * tiles.shape[0] * T**3
    sds = jax.ShapeDtypeStruct

    x_all = gather_row(node_input).reshape(G, T, T)
    first = kernel_call(
        spread_first, sds((G, 3 * T, T), B), [SMEM, SMEM, VMEM, VMEM, VMEM],
        [pltpu.VMEM((G, T, T), F)], spread_flops, "spread_first",
    )(rows, cols, tiles, x_all, logit_grad)
    received = swap(first, "col")
    sums = received[:, : 2 * T].astype(F)
    agg_in = (sums[:, :T] + sums[:, T:]).sum(0).astype(B)

    agg_all = gather_row(agg_in).reshape(G, T, T)
    pulled = kernel_call(
        spread_back, sds((G, T, T), F), [SMEM, SMEM, VMEM, VMEM],
        [pltpu.VMEM((G, T, T), B)], spread_flops, "spread_back",
    )(rows, cols, tiles, received)

    width = weight_in.shape[1]
    proj, packed = kernel_call(
        functools.partial(dense_part, scale), (sds((G, T, T), B), sds((G, 64, T), B)), [VMEM] * 5,
        [pltpu.VMEM((T, width), F), pltpu.VMEM((T, width), F)], 10 * G * T * T * width, "dense_part",
    )(agg_all, pulled, weight_in, weight_out, weight_out.T)

    packed = swap(packed, "row")
    second = kernel_call(
        spread_second, sds((G, T + 64, T), B), [SMEM, SMEM, VMEM, VMEM],
        [pltpu.VMEM((G, T, T), F)], spread_flops, "spread_second",
    )(rows, cols, tiles, proj)
    row_sum = packed.astype(F).sum(0).astype(B)
    second = second.at[:, T:].set(jnp.broadcast_to(row_sum[None], (G, 64, T)))
    second = swap(second, "col").astype(F).sum(0)
    logits = second[:T]

    slices = gather_row(second[T:].astype(B))
    w_in_grad, w_out_grad = kernel_call(
        unpack, (sds((T, width), F), sds((width, T), F)), [VMEM], [], 0, "unpack",
    )(slices)
    return (logits, w_in_grad, w_out_grad)


def solution(mesh):
    placed = (
        P(("row", "col"), None),
        P("row", "col", None, None, None),
        P("row", "col", None),
        P("row", "col", None),
        P(),
        P(),
        P(("row", "col"), None),
    )
    return jax.shard_map(
        on_device,
        mesh=mesh,
        in_specs=placed,
        out_specs=(P(("row", "col"), None), P(), P()),
        check_vma=False,
    )
```

```python
import functools
import math

import jax
import jax.numpy as jnp
from jax import lax
from jax.experimental import pallas as pl
from jax.experimental.pallas import tpu as pltpu
from jax.sharding import PartitionSpec as P

B, F = jnp.bfloat16, jnp.float32
VMEM = pl.BlockSpec(memory_space=pltpu.VMEM)
SMEM = pl.BlockSpec(memory_space=pltpu.SMEM)
ANY = pl.BlockSpec(memory_space=pl.ANY)
T = 128
G = 16
Z = 8
S = 32
UNROLL = 32
DENSE_UNROLL = 4


def kernel_call(body, name, flops, out, specs, scratch=(), limit=20):
    return pl.pallas_call(
        body,
        out_shape=out,
        in_specs=specs,
        out_specs=jax.tree.map(lambda _: VMEM, out),
        scratch_shapes=list(scratch),
        cost_estimate=pl.CostEstimate(flops=flops, bytes_accessed=6 << 20, transcendentals=0),
        compiler_params=pltpu.CompilerParams(vmem_limit_bytes=limit << 20),
        name=name,
    )


def fetch(pairs, sems):
    copies = [pltpu.make_async_copy(a, b, sems.at[i]) for i, (a, b) in enumerate(pairs)]
    for copy in copies:
        copy.start()
    return copies


def each_tile(tiles, held, sems, total, before, product, target):
    steps = tiles.shape[0] // UNROLL
    parts = [pl.ds(step * UNROLL, UNROLL) for step in range(steps)]
    arrivals = fetch([(tiles.at[part], held.at[part]) for part in parts], sems)
    total[...] = jnp.zeros_like(total)
    before()
    for step in range(steps):
        arrivals[step].wait()
        first = step * UNROLL
        terms = [product(held[first + u], first + u) for u in range(UNROLL)]
        for u in range(UNROLL):
            total[target(first + u)] += terms[u]


def spread_first(rows, cols, tiles, feats, grads, out, held, sems, ids, more, own, total):
    copies = fetch([(rows, ids.at[0]), (cols, ids.at[1]), (grads, own)], more)

    def before():
        for copy in copies:
            copy.wait()

    each_tile(
        tiles,
        held,
        sems,
        total,
        before,
        lambda tile, k: jnp.dot(tile, feats[ids[1, k]], preferred_element_type=F),
        lambda k: ids[0, k],
    )
    for i in range(G):
        out[i, 0:T] = total[i].astype(B)
        out[i, T:] = own[...]


def spread_second(rows, cols, tiles, high, low, out, held, sems, ids, more, total):
    copies = fetch([(rows, ids.at[0]), (cols, ids.at[1])], more)

    def before():
        for copy in copies:
            copy.wait()

    def product(tile, k):
        q = ids[1, k]
        twice = jnp.concatenate([tile, tile], 1)
        feats = jnp.concatenate([part[q & 1, q >> 1] for part in (high, low)], 0)
        return jnp.dot(twice, feats, preferred_element_type=F)

    each_tile(tiles, held, sems, total, before, product, lambda k: ids[0, k])
    for i in range(G):
        out[i, 0:T] = total[i].astype(B)
        out[i, T:] = jnp.zeros((S, T), B)


def spread_back(core, rows, cols, tiles, received, keep, send, held, sems, ids, more, turned, total):
    copies = fetch([(rows, ids.at[0]), (cols, ids.at[1])], more)

    def before():
        for i in range(G):
            turned[i] = received[i, T:].T
        for copy in copies:
            copy.wait()

    def target(k):
        q = ids[1, k]
        return ((q & 1) ^ core[0]) * Z + (q >> 1)

    each_tile(
        tiles,
        held,
        sems,
        total,
        before,
        lambda tile, k: jnp.dot(turned[ids[0, k]], tile, preferred_element_type=F),
        target,
    )
    keep[...] = total[:Z]
    send[...] = total[Z:].astype(B)


def collect(received, out):
    total = jnp.zeros((T, T), F)
    for i in range(G):
        total = total + received[i, 0:T].astype(F)
    total = total.astype(B)
    for z in range(Z):
        out[z] = total


def halves(value):
    high = value.astype(B)
    return high, (value - high.astype(F)).astype(B)


def product(left, right, dims=((1,), (0,))):
    return lax.dot_general(left, right, (dims, ((), ())), preferred_element_type=F)


def dense(scale, core, agg, keep, got, w_in, w_out, *refs):
    *proj, own, other, in_sum, out_sum = refs
    in_sum[...] = jnp.zeros_like(in_sum)
    out_sum[...] = jnp.zeros_like(out_sum)
    turned = w_out[...].T
    turned = jnp.concatenate([turned, turned], 0)

    def two_tiles(p):
        nodes = agg[p]
        pre = product(nodes, w_in[...])
        sig = jax.nn.sigmoid(pre)
        act = pre * sig
        high, low = halves(act)
        projected = halves(product(high, w_out[...]) + product(low, w_out[...]))
        for i in range(2):
            for part in range(2):
                proj[part][2 * p + i] = projected[part][i * T : i * T + T]
        pulled = [(keep[2 * p + i] + got[2 * p + i].astype(F)) * scale for i in range(2)]
        pull_high, pull_low = halves(jnp.concatenate(pulled, 1))
        grad = product(jnp.concatenate([pull_high, pull_low], 0), turned, ((0,), (0,)))
        grad_high, grad_low = halves(grad * (sig + act * (1.0 - sig)))
        in_term = product(nodes, grad_high, ((0,), (0,))) + product(nodes, grad_low, ((0,), (0,)))
        out_term = product(pull_high, high) + product(pull_high, low) + product(pull_low, high)
        return in_term, out_term

    def body(step, carry):
        terms = [two_tiles(step * DENSE_UNROLL + u) for u in range(DENSE_UNROLL)]
        in_sum[...] += sum(term[0] for term in terms)
        out_sum[...] += sum(term[1] for term in terms)
        return carry

    lax.fori_loop(0, Z // 2 // DENSE_UNROLL, body, 0)
    out_term = out_sum[...].T
    first = core[0] == 0
    for c in range(G):
        in_part = jnp.concatenate(
            [in_sum[8 * c : 8 * c + 8, T * b : T * b + T] for b in range(4)], 0
        )
        out_part = out_term[S * c : S * c + S]
        own[c] = jnp.where(first, in_part, out_part)
        other[c] = jnp.where(first, out_part, in_part)


def merge(own, got, out):
    out[:, 0:S], out[:, S:] = halves(own[...] + got[...])


def share(terms, unused_high, unused_low, out):
    total = jnp.zeros((S, T), F)
    for c in range(G):
        total = total + (terms[c, 0:S].astype(F) + terms[c, S:].astype(F))
    for z in range(Z):
        out[z] = total


def finish(slices, second, logits, in_grad, out_grad):
    total = second[0, 0:T].astype(F)
    for c in range(1, G):
        total = total + second[c, 0:T].astype(F)
    logits[...] = total
    for c in range(G):
        piece = slices[0, c].astype(F)
        for b in range(4):
            in_grad[8 * c : 8 * c + 8, T * b : T * b + T] = piece[8 * b : 8 * b + 8]
        out_grad[S * c : S * c + S] = slices[1, c].astype(F)


SAME_CORE = [[2 * z + core for z in range(Z)] for core in range(2)]
SAME_CHIP = [[2 * z, 2 * z + 1] for z in range(Z)]


def swap(value, axis, groups=None):
    return lax.all_to_all(value, axis, 0, 0, tiled=True, axis_index_groups=groups)


def to_all(value, count):
    return jnp.broadcast_to(value[None], (count,) + value.shape)


def both_cores(value):
    return lax.all_gather(value, "row", axis=0, axis_index_groups=SAME_CHIP)


def other_core(value):
    return lax.ppermute(value, "row", [(i, i ^ 1) for i in range(G)])


def on_device(node_input, adj_tiles, tile_row, tile_col, weight_in, weight_out, logit_grad):
    tiles = adj_tiles.reshape(-1, T, T)
    rows = tile_row.reshape(-1)
    cols = tile_col.reshape(-1)
    core = (lax.axis_index("row") % 2).reshape(1)
    scale = 1.0 / math.sqrt(node_input.shape[0] * G * G)
    spread_flops = 2 * tiles.shape[0] * T**3
    width = weight_in.shape[1]
    sds = jax.ShapeDtypeStruct
    steps = tiles.shape[0] // UNROLL
    blocks = (G, T, T)
    stream = [
        pltpu.VMEM(tiles.shape, B),
        pltpu.SemaphoreType.DMA((steps,)),
        pltpu.SMEM((2, tiles.shape[0]), jnp.int32),
        pltpu.SemaphoreType.DMA((3,)),
    ]
    rows, cols, tiles, grads = (
        pltpu.with_memory_space_constraint(array, pltpu.HBM)
        for array in (rows, cols, tiles, logit_grad)
    )

    x_all = lax.all_gather(node_input, "row", axis=0)
    first = kernel_call(
        spread_first, "spread_first", spread_flops, sds((G, 2 * T, T), B),
        [ANY, ANY, ANY, VMEM, ANY], stream + [pltpu.VMEM((T, T), B), pltpu.VMEM(blocks, F)],
    )(rows, cols, tiles, x_all, grads)
    received = swap(first, "col")
    agg = kernel_call(collect, "collect", 0, sds((Z, T, T), B), [VMEM])(received)
    agg = swap(agg, "row", SAME_CORE)
    keep, send = kernel_call(
        spread_back, "spread_back", spread_flops, (sds((Z, T, T), F), sds((Z, T, T), B)),
        [SMEM, ANY, ANY, ANY, VMEM], stream + [pltpu.VMEM(blocks, B), pltpu.VMEM(blocks, F)],
    )(core, rows, cols, tiles, received)
    got = other_core(send)

    *proj, own, other = kernel_call(
        functools.partial(dense, scale), "dense", 20 * Z * T * T * width,
        (sds((Z, T, T), B), sds((Z, T, T), B), sds((G, S, T), F), sds((G, S, T), F)),
        [SMEM] + [VMEM] * 5,
        [pltpu.VMEM((T, width), F), pltpu.VMEM((T, width), F)],
    )(core, agg.reshape(Z // 2, 2 * T, T), keep, got, weight_in, weight_out)
    terms = kernel_call(merge, "merge", 0, sds((G, 2 * S, T), B), [VMEM, VMEM])(
        own, other_core(other)
    )
    terms = swap(terms, "col")
    proj = [both_cores(part) for part in proj]
    col_sum = kernel_call(share, "share", 0, sds((Z, S, T), F), [VMEM, ANY, ANY])(terms, *proj)
    second = kernel_call(
        spread_second, "spread_second", spread_flops, sds((G, T + S, T), B),
        [ANY, ANY, ANY, VMEM, VMEM], stream + [pltpu.VMEM(blocks, F)],
    )(rows, cols, tiles, *proj)

    total = swap(col_sum, "row", SAME_CORE).sum(0).astype(B)
    second = second.at[:, T:].set(to_all(total, G))
    second = swap(second, "col")
    return kernel_call(
        finish, "finish", 0, (sds((T, T), F), sds((T, width), F), sds((width, T), F)),
        [VMEM, VMEM],
    )(both_cores(second[:, T:]), second)


def solution(mesh):
    placed = (
        P(("row", "col"), None),
        P("row", "col", None, None, None),
        P("row", "col", None),
        P("row", "col", None),
        P(),
        P(),
        P(("row", "col"), None),
    )
    return jax.shard_map(
        on_device,
        mesh=mesh,
        in_specs=placed,
        out_specs=(P(("row", "col"), None), P(), P()),
        check_vma=False,
    )
```

```python
import functools
import math

import jax
import jax.numpy as jnp
from jax import lax
from jax.experimental import pallas as pl
from jax.experimental.pallas import tpu as pltpu
from jax.sharding import PartitionSpec as P

B, F = jnp.bfloat16, jnp.float32
VMEM = pl.BlockSpec(memory_space=pltpu.VMEM)
SMEM = pl.BlockSpec(memory_space=pltpu.SMEM)
ANY = pl.BlockSpec(memory_space=pl.ANY)
T = 128
G = 16
Z = 8
S = 32
UNROLL = 64
DENSE_UNROLL = 4


def kernel_call(body, name, flops, out, specs, scratch=(), limit=20):
    return pl.pallas_call(
        body,
        out_shape=out,
        in_specs=specs,
        out_specs=jax.tree.map(lambda _: VMEM, out),
        scratch_shapes=list(scratch),
        cost_estimate=pl.CostEstimate(flops=flops, bytes_accessed=6 << 20, transcendentals=0),
        compiler_params=pltpu.CompilerParams(vmem_limit_bytes=limit << 20),
        name=name,
    )


def fetch(pairs, sems):
    copies = [pltpu.make_async_copy(a, b, sems.at[i]) for i, (a, b) in enumerate(pairs)]
    for copy in copies:
        copy.start()
    return copies


def each_tile(tiles, held, sems, total, before, product, target):
    steps = tiles.shape[0] // UNROLL
    parts = [pl.ds(step * UNROLL, UNROLL) for step in range(steps)]
    arrivals = fetch([(tiles.at[part], held.at[part]) for part in parts], sems)
    total[...] = jnp.zeros_like(total)
    before()
    for step in range(steps):
        arrivals[step].wait()
        first = step * UNROLL
        terms = [product(held[first + u], first + u) for u in range(UNROLL)]
        for u in range(UNROLL):
            total[target(first + u)] += terms[u]


def spread_first(rows, cols, tiles, feats, grads, out, held, sems, ids, more, own, total):
    copies = fetch([(rows, ids.at[0]), (cols, ids.at[1]), (grads, own)], more)

    def before():
        for copy in copies:
            copy.wait()

    each_tile(
        tiles,
        held,
        sems,
        total,
        before,
        lambda tile, k: jnp.dot(tile, feats[ids[1, k]], preferred_element_type=F),
        lambda k: ids[0, k],
    )
    for i in range(G):
        out[i, 0:T] = total[i].astype(B)
        out[i, T:] = own[...]


def spread_second(rows, cols, tiles, feats, out, held, sems, ids, more, total):
    copies = fetch([(rows, ids.at[0]), (cols, ids.at[1])], more)

    def before():
        for copy in copies:
            copy.wait()

    def product(tile, k):
        q = ids[1, k]
        return jnp.dot(tile, feats[q & 1, q >> 1], preferred_element_type=F)

    each_tile(tiles, held, sems, total, before, product, lambda k: ids[0, k])
    for i in range(G):
        out[i, 0:T] = total[i].astype(B)
        out[i, T:] = jnp.zeros((S, T), B)


def spread_back(core, rows, cols, tiles, received, keep, send, held, sems, ids, more, turned, total):
    copies = fetch([(rows, ids.at[0]), (cols, ids.at[1])], more)

    def before():
        for i in range(G):
            turned[i] = received[i, T:].T
        for copy in copies:
            copy.wait()

    def target(k):
        q = ids[1, k]
        return ((q & 1) ^ core[0]) * Z + (q >> 1)

    each_tile(
        tiles,
        held,
        sems,
        total,
        before,
        lambda tile, k: jnp.dot(turned[ids[0, k]], tile, preferred_element_type=F),
        target,
    )
    keep[...] = total[:Z]
    send[...] = total[Z:].astype(B)


def collect(received, out):
    total = jnp.zeros((T, T), F)
    for i in range(G):
        total = total + received[i, 0:T].astype(F)
    total = total.astype(B)
    for z in range(Z):
        out[z] = total


def halves(value):
    high = value.astype(B)
    return high, (value - high.astype(F)).astype(B)


def product(left, right, dims=((1,), (0,))):
    return lax.dot_general(left, right, (dims, ((), ())), preferred_element_type=F)


def dense(scale, core, agg, keep, got, w_in, w_out, *refs):
    proj, own, other, in_sum, out_sum = refs
    in_sum[...] = jnp.zeros_like(in_sum)
    out_sum[...] = jnp.zeros_like(out_sum)
    turned = w_out[...].T
    turned = jnp.concatenate([turned, turned], 0)

    def two_tiles(p):
        nodes = agg[p]
        pre = product(nodes, w_in[...])
        sig = jax.nn.sigmoid(pre)
        act = pre * sig
        high, low = halves(act)
        projected = (product(high, w_out[...]) + product(low, w_out[...])).astype(B)
        for i in range(2):
            proj[2 * p + i] = projected[i * T : i * T + T]
        pulled = [(keep[2 * p + i] + got[2 * p + i].astype(F)) * scale for i in range(2)]
        pull_high, pull_low = halves(jnp.concatenate(pulled, 1))
        grad = product(jnp.concatenate([pull_high, pull_low], 0), turned, ((0,), (0,)))
        grad_high, grad_low = halves(grad * (sig + act * (1.0 - sig)))
        in_term = product(nodes, grad_high, ((0,), (0,))) + product(nodes, grad_low, ((0,), (0,)))
        out_term = product(pull_high, high) + product(pull_high, low) + product(pull_low, high)
        return in_term, out_term

    def body(step, carry):
        terms = [two_tiles(step * DENSE_UNROLL + u) for u in range(DENSE_UNROLL)]
        in_sum[...] += sum(term[0] for term in terms)
        out_sum[...] += sum(term[1] for term in terms)
        return carry

    lax.fori_loop(0, Z // 2 // DENSE_UNROLL, body, 0)
    out_term = out_sum[...].T
    first = core[0] == 0
    for c in range(G):
        in_part = jnp.concatenate(
            [in_sum[8 * c : 8 * c + 8, T * b : T * b + T] for b in range(4)], 0
        )
        out_part = out_term[S * c : S * c + S]
        own[c] = jnp.where(first, in_part, out_part)
        other[c] = jnp.where(first, out_part, in_part)


def merge(own, got, out):
    out[:, 0:S], out[:, S:] = halves(own[...] + got[...])


def share(terms, out):
    total = jnp.zeros((S, T), F)
    for c in range(G):
        total = total + (terms[c, 0:S].astype(F) + terms[c, S:].astype(F))
    for z in range(Z):
        out[z] = total


def finish(slices, second, logits, in_grad, out_grad):
    total = second[0, 0:T].astype(F)
    for c in range(1, G):
        total = total + second[c, 0:T].astype(F)
    logits[...] = total
    for c in range(G):
        piece = slices[0, c].astype(F)
        for b in range(4):
            in_grad[8 * c : 8 * c + 8, T * b : T * b + T] = piece[8 * b : 8 * b + 8]
        out_grad[S * c : S * c + S] = slices[1, c].astype(F)


SAME_CORE = [[2 * z + core for z in range(Z)] for core in range(2)]
SAME_CHIP = [[2 * z, 2 * z + 1] for z in range(Z)]


def swap(value, axis, groups=None):
    return lax.all_to_all(value, axis, 0, 0, tiled=True, axis_index_groups=groups)


def to_all(value, count):
    return jnp.broadcast_to(value[None], (count,) + value.shape)


def both_cores(value):
    return lax.all_gather(value, "row", axis=0, axis_index_groups=SAME_CHIP)


def other_core(value):
    return lax.ppermute(value, "row", [(i, i ^ 1) for i in range(G)])


def on_device(node_input, adj_tiles, tile_row, tile_col, weight_in, weight_out, logit_grad):
    tiles = adj_tiles.reshape(-1, T, T)
    rows = tile_row.reshape(-1)
    cols = tile_col.reshape(-1)
    core = (lax.axis_index("row") % 2).reshape(1)
    scale = 1.0 / math.sqrt(node_input.shape[0] * G * G)
    spread_flops = 2 * tiles.shape[0] * T**3
    width = weight_in.shape[1]
    sds = jax.ShapeDtypeStruct
    steps = tiles.shape[0] // UNROLL
    blocks = (G, T, T)
    stream = [
        pltpu.VMEM(tiles.shape, B),
        pltpu.SemaphoreType.DMA((steps,)),
        pltpu.SMEM((2, tiles.shape[0]), jnp.int32),
        pltpu.SemaphoreType.DMA((3,)),
    ]
    rows, cols, tiles, grads = (
        pltpu.with_memory_space_constraint(array, pltpu.HBM)
        for array in (rows, cols, tiles, logit_grad)
    )

    x_all = lax.all_gather(node_input, "row", axis=0)
    first = kernel_call(
        spread_first, "spread_first", spread_flops, sds((G, 2 * T, T), B),
        [ANY, ANY, ANY, VMEM, ANY], stream + [pltpu.VMEM((T, T), B), pltpu.VMEM(blocks, F)],
    )(rows, cols, tiles, x_all, grads)
    received = swap(first, "col")
    agg = kernel_call(collect, "collect", 0, sds((Z, T, T), B), [VMEM])(received)
    agg = swap(agg, "row", SAME_CORE)
    keep, send = kernel_call(
        spread_back, "spread_back", spread_flops, (sds((Z, T, T), F), sds((Z, T, T), B)),
        [SMEM, ANY, ANY, ANY, VMEM], stream + [pltpu.VMEM(blocks, B), pltpu.VMEM(blocks, F)],
    )(core, rows, cols, tiles, received)
    got = other_core(send)

    proj, own, other = kernel_call(
        functools.partial(dense, scale), "dense", 20 * Z * T * T * width,
        (sds((Z, T, T), B), sds((G, S, T), F), sds((G, S, T), F)),
        [SMEM] + [VMEM] * 5,
        [pltpu.VMEM((T, width), F), pltpu.VMEM((T, width), F)],
    )(core, agg.reshape(Z // 2, 2 * T, T), keep, got, weight_in, weight_out)
    terms = kernel_call(merge, "merge", 0, sds((G, 2 * S, T), B), [VMEM, VMEM])(
        own, other_core(other)
    )
    terms = swap(terms, "col")
    proj = both_cores(proj)
    col_sum = kernel_call(share, "share", 0, sds((Z, S, T), F), [VMEM])(terms)
    second = kernel_call(
        spread_second, "spread_second", spread_flops, sds((G, T + S, T), B),
        [ANY, ANY, ANY, VMEM], stream + [pltpu.VMEM(blocks, F)],
    )(rows, cols, tiles, proj)

    total = swap(col_sum, "row", SAME_CORE).sum(0).astype(B)
    second = second.at[:, T:].set(to_all(total, G))
    second = swap(second, "col")
    return kernel_call(
        finish, "finish", 0, (sds((T, T), F), sds((T, width), F), sds((width, T), F)),
        [VMEM, VMEM],
    )(both_cores(second[:, T:]), second)


def solution(mesh):
    placed = (
        P(("row", "col"), None),
        P("row", "col", None, None, None),
        P("row", "col", None),
        P("row", "col", None),
        P(),
        P(),
        P(("row", "col"), None),
    )
    return jax.shard_map(
        on_device,
        mesh=mesh,
        in_specs=placed,
        out_specs=(P(("row", "col"), None), P(), P()),
        check_vma=False,
    )
```

```python
import functools
import math

import jax
import jax.numpy as jnp
from jax import lax
from jax.experimental import pallas as pl
from jax.experimental.pallas import tpu as pltpu
from jax.sharding import PartitionSpec as P

B, F = jnp.bfloat16, jnp.float32
VMEM = pl.BlockSpec(memory_space=pltpu.VMEM)
SMEM = pl.BlockSpec(memory_space=pltpu.SMEM)
ANY = pl.BlockSpec(memory_space=pl.ANY)
T = 128
G = 16
Z = 8
S = 32
UNROLL = 64
DENSE_UNROLL = 4


def kernel_call(body, name, flops, out, specs, scratch=(), limit=20):
    return pl.pallas_call(
        body,
        out_shape=out,
        in_specs=specs,
        out_specs=jax.tree.map(lambda _: VMEM, out),
        scratch_shapes=list(scratch),
        cost_estimate=pl.CostEstimate(flops=flops, bytes_accessed=6 << 20, transcendentals=0),
        compiler_params=pltpu.CompilerParams(vmem_limit_bytes=limit << 20),
        name=name,
    )


def chip_place(q):
    return ((q >> 1) & 3) * 2 + (q >> 3)


def fetch(pairs, sems):
    copies = [pltpu.make_async_copy(a, b, sems.at[i]) for i, (a, b) in enumerate(pairs)]
    for copy in copies:
        copy.start()
    return copies


def each_tile(tiles, held, sems, total, before, product, target):
    steps = tiles.shape[0] // UNROLL
    parts = [pl.ds(step * UNROLL, UNROLL) for step in range(steps)]
    arrivals = fetch([(tiles.at[part], held.at[part]) for part in parts], sems)
    total[...] = jnp.zeros_like(total)
    before()
    for step in range(steps):
        arrivals[step].wait()
        first = step * UNROLL
        terms = [product(held[first + u], first + u) for u in range(UNROLL)]
        for u in range(UNROLL):
            total[target(first + u)] += terms[u]


def spread_first(rows, cols, tiles, feats, grads, out, held, sems, ids, more, own, total):
    copies = fetch([(rows, ids.at[0]), (cols, ids.at[1]), (grads, own)], more)

    def before():
        for copy in copies:
            copy.wait()

    each_tile(
        tiles,
        held,
        sems,
        total,
        before,
        lambda tile, k: jnp.dot(tile, feats[ids[1, k]], preferred_element_type=F),
        lambda k: ids[0, k],
    )
    for i in range(G):
        out[i, 0:T] = total[i].astype(B)
        out[i, T:] = own[...]


def spread_second(rows, cols, tiles, feats, out, held, sems, ids, more, total):
    copies = fetch([(rows, ids.at[0]), (cols, ids.at[1])], more)

    def before():
        for copy in copies:
            copy.wait()

    def product(tile, k):
        q = ids[1, k]
        return jnp.dot(tile, feats[q & 1, chip_place(q)], preferred_element_type=F)

    each_tile(tiles, held, sems, total, before, product, lambda k: ids[0, k])
    for i in range(G):
        out[i, 0:T] = total[i].astype(B)
        out[i, T:] = jnp.zeros((S, T), B)


def spread_back(core, rows, cols, tiles, received, keep, send, held, sems, ids, more, turned, total):
    copies = fetch([(rows, ids.at[0]), (cols, ids.at[1])], more)

    def before():
        for i in range(G):
            turned[i] = received[i, T:].T
        for copy in copies:
            copy.wait()

    def target(k):
        q = ids[1, k]
        return ((q & 1) ^ core[0]) * Z + chip_place(q)

    each_tile(
        tiles,
        held,
        sems,
        total,
        before,
        lambda tile, k: jnp.dot(turned[ids[0, k]], tile, preferred_element_type=F),
        target,
    )
    keep[...] = total[:Z]
    send[...] = total[Z:].astype(B)


def collect(received, out):
    total = jnp.zeros((T, T), F)
    for i in range(G):
        total = total + received[i, 0:T].astype(F)
    total = total.astype(B)
    for z in range(Z):
        out[z] = total


def halves(value):
    high = value.astype(B)
    return high, (value - high.astype(F)).astype(B)


def product(left, right, dims=((1,), (0,))):
    return lax.dot_general(left, right, (dims, ((), ())), preferred_element_type=F)


def dense(scale, core, agg, keep, got, w_in, w_out, *refs):
    proj, own, other, in_sum, out_sum = refs
    in_sum[...] = jnp.zeros_like(in_sum)
    out_sum[...] = jnp.zeros_like(out_sum)
    turned = w_out[...].T
    turned = jnp.concatenate([turned, turned], 0)

    def two_tiles(p):
        nodes = agg[p]
        pre = product(nodes, w_in[...])
        sig = jax.nn.sigmoid(pre)
        act = pre * sig
        high, low = halves(act)
        projected = (product(high, w_out[...]) + product(low, w_out[...])).astype(B)
        for i in range(2):
            proj[2 * p + i] = projected[i * T : i * T + T]
        pulled = [(keep[2 * p + i] + got[2 * p + i].astype(F)) * scale for i in range(2)]
        pull_high, pull_low = halves(jnp.concatenate(pulled, 1))
        grad = product(jnp.concatenate([pull_high, pull_low], 0), turned, ((0,), (0,)))
        grad_high, grad_low = halves(grad * (sig + act * (1.0 - sig)))
        in_term = product(nodes, grad_high, ((0,), (0,))) + product(nodes, grad_low, ((0,), (0,)))
        out_term = product(pull_high, high) + product(pull_high, low) + product(pull_low, high)
        return in_term, out_term

    def body(step, carry):
        terms = [two_tiles(step * DENSE_UNROLL + u) for u in range(DENSE_UNROLL)]
        in_sum[...] += sum(term[0] for term in terms)
        out_sum[...] += sum(term[1] for term in terms)
        return carry

    lax.fori_loop(0, Z // 2 // DENSE_UNROLL, body, 0)
    out_term = out_sum[...].T
    first = core[0] == 0
    for c in range(G):
        in_part = jnp.concatenate(
            [in_sum[8 * c : 8 * c + 8, T * b : T * b + T] for b in range(4)], 0
        )
        out_part = out_term[S * c : S * c + S]
        own[c] = jnp.where(first, in_part, out_part)
        other[c] = jnp.where(first, out_part, in_part)


def merge(own, got, out):
    out[:, 0:S], out[:, S:] = halves(own[...] + got[...])


def share(terms, out):
    total = jnp.zeros((S, T), F)
    for c in range(G):
        total = total + (terms[c, 0:S].astype(F) + terms[c, S:].astype(F))
    for z in range(Z):
        out[z] = total


def finish(slices, second, logits, in_grad, out_grad):
    total = second[0, 0:T].astype(F)
    for c in range(1, G):
        total = total + second[c, 0:T].astype(F)
    logits[...] = total
    for c in range(G):
        piece = slices[0, c].astype(F)
        for b in range(4):
            in_grad[8 * c : 8 * c + 8, T * b : T * b + T] = piece[8 * b : 8 * b + 8]
        out_grad[S * c : S * c + S] = slices[1, c].astype(F)


SAME_CORE = [[2 * z + core for z in (0, 4, 1, 5, 2, 6, 3, 7)] for core in range(2)]
SAME_CHIP = [[2 * z, 2 * z + 1] for z in range(Z)]


def swap(value, axis, groups=None):
    return lax.all_to_all(value, axis, 0, 0, tiled=True, axis_index_groups=groups)


def to_all(value, count):
    return jnp.broadcast_to(value[None], (count,) + value.shape)


def both_cores(value):
    return lax.all_gather(value, "row", axis=0, axis_index_groups=SAME_CHIP)


def other_core(value):
    return lax.ppermute(value, "row", [(i, i ^ 1) for i in range(G)])


def on_device(node_input, adj_tiles, tile_row, tile_col, weight_in, weight_out, logit_grad):
    tiles = adj_tiles.reshape(-1, T, T)
    rows = tile_row.reshape(-1)
    cols = tile_col.reshape(-1)
    core = (lax.axis_index("row") % 2).reshape(1)
    scale = 1.0 / math.sqrt(node_input.shape[0] * G * G)
    spread_flops = 2 * tiles.shape[0] * T**3
    width = weight_in.shape[1]
    sds = jax.ShapeDtypeStruct
    steps = tiles.shape[0] // UNROLL
    blocks = (G, T, T)
    stream = [
        pltpu.VMEM(tiles.shape, B),
        pltpu.SemaphoreType.DMA((steps,)),
        pltpu.SMEM((2, tiles.shape[0]), jnp.int32),
        pltpu.SemaphoreType.DMA((3,)),
    ]
    rows, cols, tiles, grads = (
        pltpu.with_memory_space_constraint(array, pltpu.HBM)
        for array in (rows, cols, tiles, logit_grad)
    )

    x_all = lax.all_gather(node_input, "row", axis=0)
    first = kernel_call(
        spread_first, "spread_first", spread_flops, sds((G, 2 * T, T), B),
        [ANY, ANY, ANY, VMEM, ANY], stream + [pltpu.VMEM((T, T), B), pltpu.VMEM(blocks, F)],
    )(rows, cols, tiles, x_all, grads)
    received = swap(first, "col")
    agg = kernel_call(collect, "collect", 0, sds((Z, T, T), B), [VMEM])(received)
    agg = swap(agg, "row", SAME_CORE)
    keep, send = kernel_call(
        spread_back, "spread_back", spread_flops, (sds((Z, T, T), F), sds((Z, T, T), B)),
        [SMEM, ANY, ANY, ANY, VMEM], stream + [pltpu.VMEM(blocks, B), pltpu.VMEM(blocks, F)],
    )(core, rows, cols, tiles, received)
    got = other_core(send)

    proj, own, other = kernel_call(
        functools.partial(dense, scale), "dense", 20 * Z * T * T * width,
        (sds((Z, T, T), B), sds((G, S, T), F), sds((G, S, T), F)),
        [SMEM] + [VMEM] * 5,
        [pltpu.VMEM((T, width), F), pltpu.VMEM((T, width), F)],
    )(core, agg.reshape(Z // 2, 2 * T, T), keep, got, weight_in, weight_out)
    terms = kernel_call(merge, "merge", 0, sds((G, 2 * S, T), B), [VMEM, VMEM])(
        own, other_core(other)
    )
    terms = swap(terms, "col")
    proj = both_cores(proj)
    col_sum = kernel_call(share, "share", 0, sds((Z, S, T), F), [VMEM])(terms)
    second = kernel_call(
        spread_second, "spread_second", spread_flops, sds((G, T + S, T), B),
        [ANY, ANY, ANY, VMEM], stream + [pltpu.VMEM(blocks, F)],
    )(rows, cols, tiles, proj)

    total = swap(col_sum, "row", SAME_CORE).sum(0).astype(B)
    second = second.at[:, T:].set(to_all(total, G))
    second = swap(second, "col")
    return kernel_call(
        finish, "finish", 0, (sds((T, T), F), sds((T, width), F), sds((width, T), F)),
        [VMEM, VMEM],
    )(both_cores(second[:, T:]), second)


def solution(mesh):
    placed = (
        P(("row", "col"), None),
        P("row", "col", None, None, None),
        P("row", "col", None),
        P("row", "col", None),
        P(),
        P(),
        P(("row", "col"), None),
    )
    return jax.shard_map(
        on_device,
        mesh=mesh,
        in_specs=placed,
        out_specs=(P(("row", "col"), None), P(), P()),
        check_vma=False,
    )
```

```python
import functools
import math

import jax
import jax.numpy as jnp
from jax import lax
from jax.experimental import pallas as pl
from jax.experimental.pallas import tpu as pltpu
from jax.sharding import PartitionSpec as P

B, F = jnp.bfloat16, jnp.float32
VMEM = pl.BlockSpec(memory_space=pltpu.VMEM)
SMEM = pl.BlockSpec(memory_space=pltpu.SMEM)
ANY = pl.BlockSpec(memory_space=pl.ANY)
T = 128
G = 16
Z = 8
S = 32
UNROLL = 64
DENSE_UNROLL = 4


def kernel_call(body, name, flops, out, specs, scratch=(), limit=20):
    return pl.pallas_call(
        body,
        out_shape=out,
        in_specs=specs,
        out_specs=jax.tree.map(lambda _: VMEM, out),
        scratch_shapes=list(scratch),
        cost_estimate=pl.CostEstimate(flops=flops, bytes_accessed=6 << 20, transcendentals=0),
        compiler_params=pltpu.CompilerParams(vmem_limit_bytes=limit << 20),
        name=name,
    )


def chip_place(q):
    return ((q >> 1) & 1) * 4 + ((q >> 1) & 2) + (q >> 3)


def fetch(pairs, sems):
    copies = [pltpu.make_async_copy(a, b, sems.at[i]) for i, (a, b) in enumerate(pairs)]
    for copy in copies:
        copy.start()
    return copies


def each_tile(tiles, held, sems, total, before, product, target):
    steps = tiles.shape[0] // UNROLL
    parts = [pl.ds(step * UNROLL, UNROLL) for step in range(steps)]
    arrivals = fetch([(tiles.at[part], held.at[part]) for part in parts], sems)
    total[...] = jnp.zeros_like(total)
    before()
    for step in range(steps):
        arrivals[step].wait()
        first = step * UNROLL
        terms = [product(held[first + u], first + u) for u in range(UNROLL)]
        for u in range(UNROLL):
            total[target(first + u)] += terms[u]


def spread_first(rows, cols, tiles, feats, grads, out, held, sems, ids, more, own, total):
    copies = fetch([(rows, ids.at[0]), (cols, ids.at[1]), (grads, own)], more)

    def before():
        for copy in copies:
            copy.wait()

    each_tile(
        tiles,
        held,
        sems,
        total,
        before,
        lambda tile, k: jnp.dot(tile, feats[ids[1, k]], preferred_element_type=F),
        lambda k: ids[0, k],
    )
    for i in range(G):
        out[i, 0:T] = total[i].astype(B)
        out[i, T:] = own[...]


def spread_second(rows, cols, tiles, feats, out, held, sems, ids, more, total):
    copies = fetch([(rows, ids.at[0]), (cols, ids.at[1])], more)

    def before():
        for copy in copies:
            copy.wait()

    def product(tile, k):
        q = ids[1, k]
        return jnp.dot(tile, feats[q & 1, chip_place(q)], preferred_element_type=F)

    each_tile(tiles, held, sems, total, before, product, lambda k: ids[0, k])
    for i in range(G):
        out[i, 0:T] = total[i].astype(B)
        out[i, T:] = jnp.zeros((S, T), B)


def spread_back(core, rows, cols, tiles, received, keep, send, held, sems, ids, more, turned, total):
    copies = fetch([(rows, ids.at[0]), (cols, ids.at[1])], more)

    def before():
        for i in range(G):
            turned[i] = received[i, T:].T
        for copy in copies:
            copy.wait()

    def target(k):
        q = ids[1, k]
        return ((q & 1) ^ core[0]) * Z + chip_place(q)

    each_tile(
        tiles,
        held,
        sems,
        total,
        before,
        lambda tile, k: jnp.dot(turned[ids[0, k]], tile, preferred_element_type=F),
        target,
    )
    keep[...] = total[:Z]
    send[...] = total[Z:].astype(B)


def collect(received, out):
    total = jnp.zeros((T, T), F)
    for i in range(G):
        total = total + received[i, 0:T].astype(F)
    total = total.astype(B)
    for z in range(Z):
        out[z] = total


def halves(value):
    high = value.astype(B)
    return high, (value - high.astype(F)).astype(B)


def product(left, right, dims=((1,), (0,))):
    return lax.dot_general(left, right, (dims, ((), ())), preferred_element_type=F)


def dense(scale, core, agg, keep, got, w_in, w_out, *refs):
    proj, own, other, in_sum, out_sum = refs
    in_sum[...] = jnp.zeros_like(in_sum)
    out_sum[...] = jnp.zeros_like(out_sum)
    turned = w_out[...].T
    turned = jnp.concatenate([turned, turned], 0)

    def two_tiles(p):
        nodes = agg[p]
        pre = product(nodes, w_in[...])
        sig = jax.nn.sigmoid(pre)
        act = pre * sig
        high, low = halves(act)
        projected = (product(high, w_out[...]) + product(low, w_out[...])).astype(B)
        for i in range(2):
            proj[2 * p + i] = projected[i * T : i * T + T]
        pulled = [(keep[2 * p + i] + got[2 * p + i].astype(F)) * scale for i in range(2)]
        pull_high, pull_low = halves(jnp.concatenate(pulled, 1))
        grad = product(jnp.concatenate([pull_high, pull_low], 0), turned, ((0,), (0,)))
        grad_high, grad_low = halves(grad * (sig + act * (1.0 - sig)))
        in_term = product(nodes, grad_high, ((0,), (0,))) + product(nodes, grad_low, ((0,), (0,)))
        out_term = product(pull_high, high) + product(pull_high, low) + product(pull_low, high)
        return in_term, out_term

    def body(step, carry):
        terms = [two_tiles(step * DENSE_UNROLL + u) for u in range(DENSE_UNROLL)]
        in_sum[...] += sum(term[0] for term in terms)
        out_sum[...] += sum(term[1] for term in terms)
        return carry

    lax.fori_loop(0, Z // 2 // DENSE_UNROLL, body, 0)
    out_term = out_sum[...].T
    first = core[0] == 0
    for c in range(G):
        in_part = jnp.concatenate(
            [in_sum[8 * c : 8 * c + 8, T * b : T * b + T] for b in range(4)], 0
        )
        out_part = out_term[S * c : S * c + S]
        own[c] = jnp.where(first, in_part, out_part)
        other[c] = jnp.where(first, out_part, in_part)


def merge(own, got, out):
    out[:, 0:S], out[:, S:] = halves(own[...] + got[...])


def share(terms, out):
    total = jnp.zeros((S, T), F)
    for c in range(G):
        total = total + (terms[c, 0:S].astype(F) + terms[c, S:].astype(F))
    for z in range(Z):
        out[z] = total


def finish(slices, second, logits, in_grad, out_grad):
    total = second[0, 0:T].astype(F)
    for c in range(1, G):
        total = total + second[c, 0:T].astype(F)
    logits[...] = total
    for c in range(G):
        piece = slices[0, c].astype(F)
        for b in range(4):
            in_grad[8 * c : 8 * c + 8, T * b : T * b + T] = piece[8 * b : 8 * b + 8]
        out_grad[S * c : S * c + S] = slices[1, c].astype(F)


SAME_CORE = [[2 * z + core for z in (0, 4, 2, 6, 1, 5, 3, 7)] for core in range(2)]
SAME_CHIP = [[2 * z, 2 * z + 1] for z in range(Z)]


def swap(value, axis, groups=None):
    return lax.all_to_all(value, axis, 0, 0, tiled=True, axis_index_groups=groups)


def to_all(value, count):
    return jnp.broadcast_to(value[None], (count,) + value.shape)


def both_cores(value):
    return lax.all_gather(value, "row", axis=0, axis_index_groups=SAME_CHIP)


def other_core(value):
    return lax.ppermute(value, "row", [(i, i ^ 1) for i in range(G)])


def on_device(node_input, adj_tiles, tile_row, tile_col, weight_in, weight_out, logit_grad):
    tiles = adj_tiles.reshape(-1, T, T)
    rows = tile_row.reshape(-1)
    cols = tile_col.reshape(-1)
    core = (lax.axis_index("row") % 2).reshape(1)
    scale = 1.0 / math.sqrt(node_input.shape[0] * G * G)
    spread_flops = 2 * tiles.shape[0] * T**3
    width = weight_in.shape[1]
    sds = jax.ShapeDtypeStruct
    steps = tiles.shape[0] // UNROLL
    blocks = (G, T, T)
    stream = [
        pltpu.VMEM(tiles.shape, B),
        pltpu.SemaphoreType.DMA((steps,)),
        pltpu.SMEM((2, tiles.shape[0]), jnp.int32),
        pltpu.SemaphoreType.DMA((3,)),
    ]
    rows, cols, tiles, grads = (
        pltpu.with_memory_space_constraint(array, pltpu.HBM)
        for array in (rows, cols, tiles, logit_grad)
    )

    x_all = lax.all_gather(node_input, "row", axis=0)
    first = kernel_call(
        spread_first, "spread_first", spread_flops, sds((G, 2 * T, T), B),
        [ANY, ANY, ANY, VMEM, ANY], stream + [pltpu.VMEM((T, T), B), pltpu.VMEM(blocks, F)],
    )(rows, cols, tiles, x_all, grads)
    received = swap(first, "col")
    agg = kernel_call(collect, "collect", 0, sds((Z, T, T), B), [VMEM])(received)
    agg = swap(agg, "row", SAME_CORE)
    keep, send = kernel_call(
        spread_back, "spread_back", spread_flops, (sds((Z, T, T), F), sds((Z, T, T), B)),
        [SMEM, ANY, ANY, ANY, VMEM], stream + [pltpu.VMEM(blocks, B), pltpu.VMEM(blocks, F)],
    )(core, rows, cols, tiles, received)
    got = other_core(send)

    proj, own, other = kernel_call(
        functools.partial(dense, scale), "dense", 20 * Z * T * T * width,
        (sds((Z, T, T), B), sds((G, S, T), F), sds((G, S, T), F)),
        [SMEM] + [VMEM] * 5,
        [pltpu.VMEM((T, width), F), pltpu.VMEM((T, width), F)],
    )(core, agg.reshape(Z // 2, 2 * T, T), keep, got, weight_in, weight_out)
    terms = kernel_call(merge, "merge", 0, sds((G, 2 * S, T), B), [VMEM, VMEM])(
        own, other_core(other)
    )
    terms = swap(terms, "col")
    proj = both_cores(proj)
    col_sum = kernel_call(share, "share", 0, sds((Z, S, T), F), [VMEM])(terms)
    second = kernel_call(
        spread_second, "spread_second", spread_flops, sds((G, T + S, T), B),
        [ANY, ANY, ANY, VMEM], stream + [pltpu.VMEM(blocks, F)],
    )(rows, cols, tiles, proj)

    total = swap(col_sum, "row", SAME_CORE).sum(0).astype(B)
    second = second.at[:, T:].set(to_all(total, G))
    second = swap(second, "col")
    return kernel_call(
        finish, "finish", 0, (sds((T, T), F), sds((T, width), F), sds((width, T), F)),
        [VMEM, VMEM],
    )(both_cores(second[:, T:]), second)


def solution(mesh):
    placed = (
        P(("row", "col"), None),
        P("row", "col", None, None, None),
        P("row", "col", None),
        P("row", "col", None),
        P(),
        P(),
        P(("row", "col"), None),
    )
    return jax.shard_map(
        on_device,
        mesh=mesh,
        in_specs=placed,
        out_specs=(P(("row", "col"), None), P(), P()),
        check_vma=False,
    )
```
